32 devices in a mesh: ctx: 4 (over y, x), head: 2 (over core), dp: 4 (over z).
Axes of the slice: x: 2, y: 2, z: 4, core: 2. Of those that a mesh axis runs over, the one named last changes fastest.
Arguments:
- query_raw: bfloat16 [4, 512, 4096], P('dp', 'ctx', 'head'), may hold values from -6 to 6
- key_raw: bfloat16 [4, 512, 512], P('dp', 'ctx', 'head'), may hold values from -6 to 6
- value_rows: bfloat16 [4, 512, 512], P('dp', 'ctx', 'head'), may hold values from -6 to 6
- attn_out: bfloat16 [4, 512, 4096], P('dp', 'ctx', 'head'), may hold values from -2 to 2
- out_grad: bfloat16 [4, 512, 4096], P('dp', 'ctx', 'head'), may hold values from -6 to 6
- log_totals: float32 [4, 32, 512], P('dp', 'head', 'ctx'), may hold values from -40 to 40, as said below
- query_gain: float32 [128], replicated, may hold values from 0.5 to 1.5
- key_gain: float32 [128], replicated, may hold values from 0.5 to 1.5
Outputs:
- grad_query: float32 [4, 512, 4096], P('dp', 'ctx', 'head')
- grad_key: float32 [4, 512, 512], P('dp', 'ctx', 'head')
- grad_value: float32 [4, 512, 512], P('dp', 'ctx', 'head')
- gain_grads: float32 [2, 128], replicated
The draws below stay inside these ranges and needn't reach their ends.
Inputs may be any that keep to these rules, and one draw needn't show every extreme that they name: log_totals[s, h, i] is the log of the sum over j <= i of exp(score[i, j]) for query head h, computed from query_raw, key_raw and the gains.
All inputs are finite; a program needn't handle non-finite values.
Results may differ from the reference program's by a relative error of at most 0.009.
Values may be sent and summed in bfloat16 or wider, within the bound.
A program may use at most 64 MiB of HBM per device.

```python
import math
import jax
import jax.numpy as jnp
from jax import lax

HD = 128
HEADS = 32
KV_HEADS = 4
TOK_DEV = 128
LENGTH = 512
SEQS = 4
N_CTX = 4


def shared_draw(key):
    query_shape = (SEQS, LENGTH, HEADS * HD)
    key_shape = (SEQS, LENGTH, KV_HEADS * HD)
    query_values = jnp.clip(jax.random.normal(jax.random.fold_in(key, 101), query_shape, jnp.float32), -5.5, 5.5)
    key_values = jnp.clip(jax.random.normal(jax.random.fold_in(key, 102), key_shape, jnp.float32), -5.5, 5.5)
    query_values = query_values.astype(jnp.bfloat16)
    key_values = key_values.astype(jnp.bfloat16)
    query_gain = jax.random.uniform(jax.random.fold_in(key, 103), (HD,), jnp.float32, 0.5, 1.5)
    key_gain = jax.random.uniform(jax.random.fold_in(key, 104), (HD,), jnp.float32, 0.5, 1.5)
    logit_scale = 1.0 / math.sqrt(HD)
    group = HEADS // KV_HEADS
    positions = jnp.arange(LENGTH)
    causal = positions[:, None] >= positions[None, :]

    def normed(raw_rows, norm_gain, count):
        values = raw_rows.astype(jnp.float32).reshape(LENGTH, count, HD)
        inverse = lax.rsqrt(jnp.mean(values * values, axis=-1, keepdims=True) + 1e-06)
        return (values * inverse * norm_gain).astype(jnp.bfloat16).astype(jnp.float32)

    def one_group(inputs):
        grouped_queries, grouped_keys = inputs
        attention_logits = jnp.einsum('gqd,kd->gqk', grouped_queries, grouped_keys) * logit_scale
        masked = jnp.where(causal[None], attention_logits, -jnp.inf)
        highest = jnp.max(masked, axis=-1, keepdims=True)
        return highest[:, :, 0] + jnp.log(jnp.sum(jnp.exp(masked - highest), axis=-1))

    def one_sequence(inputs):
        query_seq, key_seq = inputs
        q_groups = normed(query_seq, query_gain, HEADS).reshape(LENGTH, KV_HEADS, group, HD).transpose(1, 2, 0, 3)
        k_groups = normed(key_seq, key_gain, KV_HEADS).transpose(1, 0, 2)
        return lax.map(one_group, (q_groups, k_groups)).reshape(HEADS, LENGTH)
    totals = lax.map(one_sequence, (query_values, key_values))
    return (query_values, key_values, query_gain, key_gain, totals)


def draw_query_raw(key, part):
    return shared_draw(key)[0]


def draw_key_raw(key, part):
    return shared_draw(key)[1]


def draw_query_gain(key, part):
    return shared_draw(key)[2]


def draw_key_gain(key, part):
    return shared_draw(key)[3]


def draw_log_totals(key, part):
    return shared_draw(key)[4]


def block_levels(stream_key, extent, split, low, largest):
    def one(axis_at, blocks):
        steps = jax.random.uniform(jax.random.fold_in(jax.random.fold_in(stream_key, 6), axis_at), (blocks,), jnp.float32, low / len(split), largest / len(split))
        return jnp.repeat(jnp.exp(steps), extent[axis_at] // blocks).reshape((-1,) + (1,) * (len(extent) - axis_at - 1))

    level = one(*split[0])
    for cut in split[1:]:
        level = level * one(*cut)
    return level


def scatter_about(key, dims, scale, limit, pieces=(), held_as=jnp.bfloat16):
    level = block_levels(key, dims, pieces, -0.22, 0.18) if pieces else 1.0
    entries = jax.random.normal(key, dims, jnp.float32) * scale * level
    return jnp.minimum(jnp.maximum(entries, -limit), limit).astype(held_as)


def setup_inputs(seed: int = 0) -> dict:
    key_list = jax.random.split(jax.random.key(seed), 9)
    query_raw = draw_query_raw(jax.random.fold_in(key_list[8], 71), 0)
    key_raw = draw_key_raw(jax.random.fold_in(key_list[8], 71), 0)
    value_rows = scatter_about(key_list[2], (SEQS, LENGTH, KV_HEADS * HD), 1.0, 6.0, ((0, 4), (1, 4), (2, 2)))
    attn_out = scatter_about(key_list[3], (SEQS, LENGTH, HEADS * HD), 0.3, 2.0, ((0, 4), (1, 4), (2, 2)))
    out_grad = scatter_about(key_list[4], (SEQS, LENGTH, HEADS * HD), 1.0, 6.0, ((0, 4), (1, 4), (2, 2)))
    log_totals = draw_log_totals(jax.random.fold_in(key_list[8], 71), 0)
    query_gain = draw_query_gain(jax.random.fold_in(key_list[8], 71), 0)
    key_gain = draw_key_gain(jax.random.fold_in(key_list[8], 71), 0)
    return dict(query_raw=query_raw, key_raw=key_raw, value_rows=value_rows, attn_out=attn_out, out_grad=out_grad, log_totals=log_totals, query_gain=query_gain, key_gain=key_gain)


def normalize(raw_rows, norm_gain):
    values = raw_rows.astype(jnp.float32).reshape(raw_rows.shape[:-1] + (-1, HD))
    inverse = lax.rsqrt(lax.optimization_barrier(jnp.mean(values * values, axis=-1, keepdims=True)) + 1e-06)
    unit_rows = values * inverse
    return (unit_rows, inverse, (unit_rows * norm_gain).astype(jnp.bfloat16))

def norm_back(grad_norm, unit_rows, inverse, norm_gain):
    grad_unit = grad_norm * norm_gain
    grad_raw = (grad_unit - unit_rows * lax.optimization_barrier(jnp.mean(grad_unit * unit_rows, axis=-1, keepdims=True))) * inverse
    return (grad_raw, lax.optimization_barrier(jnp.sum(grad_norm * unit_rows, axis=(0, 1))))

def rounded_values(values):
    return lax.optimization_barrier(values.astype(jnp.bfloat16)).astype(jnp.float32)

def reference(query_raw, key_raw, value_rows, attn_out, out_grad, log_totals, query_gain, key_gain):
    blocks = N_CTX
    rows = TOK_DEV
    group = HEADS // KV_HEADS
    logit_scale = 1.0 / math.sqrt(HD)
    positions = jnp.arange(LENGTH).reshape(blocks, rows)
    causal = positions[:, :, None, None] >= positions[None, None, :, :]

    def one_group(inputs):
        grouped_queries, grouped_keys, grouped_values, output_grad_group, d_group, t_group = inputs
        attention_logits = jnp.einsum('vcow,ziw->ovczi', grouped_queries, grouped_keys) * logit_scale
        probs = jnp.where(causal[None], jnp.exp(attention_logits - t_group[:, :, :, None, None]), 0.0)
        probs_low = rounded_values(probs)
        value_parts = rounded_values(jnp.einsum('gaqbk,aqgd->abkd', probs_low, output_grad_group))
        grad_value = lax.optimization_barrier(jnp.sum(value_parts, axis=0)).reshape(LENGTH, HD)
        probability_gradient = jnp.einsum('vcow,ziw->ovczi', output_grad_group, grouped_values)
        score_gradient = rounded_values(probs * (probability_gradient - d_group.transpose(2, 0, 1)[:, :, :, None, None]))
        query_pieces = rounded_values(jnp.einsum('vlhsr,srn->lshvn', score_gradient, grouped_keys) * logit_scale)
        key_parts = rounded_values(jnp.einsum('gaqbk,aqgd->abkd', score_gradient, grouped_queries) * logit_scale)
        grad_q = lax.optimization_barrier(jnp.sum(query_pieces, axis=1)).reshape(LENGTH, group, HD)
        grad_k = lax.optimization_barrier(jnp.sum(key_parts, axis=0)).reshape(LENGTH, HD)
        return (grad_q, grad_k, grad_value)

    def one_sequence(inputs):
        query_seq, key_seq, value_seq, output_seq, grad_seq, totals_seq = inputs
        q_unit, q_inverse, q_norm = normalize(query_seq, query_gain)
        k_unit, k_inverse, k_norm = normalize(key_seq, key_gain)
        q_blocks = q_norm.astype(jnp.float32).reshape(blocks, rows, KV_HEADS, group, HD).transpose(2, 0, 1, 3, 4)
        g_blocks = grad_seq.astype(jnp.float32).reshape(blocks, rows, KV_HEADS, group, HD).transpose(2, 0, 1, 3, 4)
        o_blocks = output_seq.astype(jnp.float32).reshape(blocks, rows, KV_HEADS, group, HD).transpose(2, 0, 1, 3, 4)
        d_blocks = lax.optimization_barrier(jnp.sum(g_blocks * o_blocks, axis=-1))
        k_blocks = k_norm.astype(jnp.float32).reshape(blocks, rows, KV_HEADS, HD).transpose(2, 0, 1, 3)
        v_blocks = value_seq.astype(jnp.float32).reshape(blocks, rows, KV_HEADS, HD).transpose(2, 0, 1, 3)
        totals = totals_seq.reshape(KV_HEADS, group, blocks, rows)
        grad_q, grad_k, grad_v = lax.map(one_group, (q_blocks, k_blocks, v_blocks, g_blocks, d_blocks, totals))
        grad_q_norm = grad_q.transpose(1, 0, 2, 3).reshape(LENGTH, HEADS, HD)
        grad_k_norm = grad_k.transpose(1, 0, 2)
        grad_value = grad_v.transpose(1, 0, 2).reshape(LENGTH, KV_HEADS * HD)
        grad_query, q_gain_sum = norm_back(grad_q_norm, q_unit, q_inverse, query_gain)
        grad_key, k_gain_sum = norm_back(grad_k_norm, k_unit, k_inverse, key_gain)
        return (grad_query.reshape(LENGTH, HEADS * HD), grad_key.reshape(LENGTH, KV_HEADS * HD), grad_value, q_gain_sum, k_gain_sum)
    grad_query, grad_key, grad_value, q_sums, k_sums = lax.map(one_sequence, (query_raw, key_raw, value_rows, attn_out, out_grad, log_totals))
    factor = 1.0 / math.sqrt(SEQS * LENGTH * HEADS)
    gain_grads = jnp.stack([lax.optimization_barrier(jnp.sum(q_sums, axis=0)), lax.optimization_barrier(jnp.sum(k_sums, axis=0))]) * factor
    return (grad_query, grad_key, grad_value, gain_grads)
```

```python
import functools
import math

import jax
import jax.numpy as jnp
from jax import lax
from jax.experimental import pallas as pl
from jax.experimental.pallas import tpu as pltpu
from jax.sharding import PartitionSpec as P

HD = 128
F32 = jnp.float32
BF16 = jnp.bfloat16
MESH = pl.DeviceIdType.MESH
LOG2E = math.log2(math.e)


def dot(a, b):
    return jnp.dot(a, b, preferred_element_type=F32)


def kernel(
    n_ctx, n_head, n_dp, gain_scale,
    q_hbm, k_hbm, v_hbm, o_hbm, g_hbm, lt_hbm, qg_hbm, kg_hbm,
    gq_ref, gk_ref, gv_ref, gain_ref,
    q_v, o_v, g_v, lt_v, qg_v, kg_v,
    kbuf, vbuf, part_out, part_in,
    unit_t, inv_s, qn_t, qn_s, g_t, delta_s, lt2_s, dq_t, gcol_s, ksum_s, buf_a, buf_b,
    in_sem, kv_send, kv_recv, p_send, p_recv, a_send, a_recv, b_send, b_recv,
):
    rows, width = q_v.shape
    heads = width // HD
    kv_width = k_hbm.shape[1]
    kv_count = kv_width // HD
    group = heads // kv_count
    chunk = math.gcd(group, 2)
    scale = 1.0 / math.sqrt(HD)
    me = lax.axis_index("ctx")
    my_head = lax.axis_index("head")
    my_dp = lax.axis_index("dp")
    n_plane = n_ctx * n_head
    my_plane = me * n_head + my_head

    loads = [
        pltpu.make_async_copy(src, dst, in_sem.at[i])
        for i, (src, dst) in enumerate(
            [
                (k_hbm, kbuf.at[me]), (v_hbm, vbuf.at[me]), (lt_hbm, lt_v), (qg_hbm, qg_v),
                (kg_hbm, kg_v), (q_hbm, q_v), (g_hbm, g_v), (o_hbm, o_v),
            ]
        )
    ]
    for load in loads:
        load.start()

    def plane_id(t):
        p = lax.rem(my_plane + t, n_plane)
        return p, {"ctx": p // n_head, "head": lax.rem(p, n_head)}

    barrier = pltpu.get_barrier_semaphore()
    for t in range(1, n_plane):
        pl.semaphore_signal(barrier, inc=1, device_id=plane_id(t)[1], device_id_type=MESH)
    for t in range(1, n_dp):
        pl.semaphore_signal(
            barrier, inc=1, device_id={"dp": lax.rem(my_dp + t, n_dp)}, device_id_type=MESH
        )
    pl.semaphore_wait(barrier, n_plane + n_dp - 2)

    def kv_copy(which, slot, other):
        return pltpu.make_async_remote_copy(
            src_ref=(k_hbm, v_hbm)[which],
            dst_ref=(kbuf, vbuf)[which].at[slot],
            send_sem=kv_send.at[which, other],
            recv_sem=kv_recv.at[which, slot],
            device_id={"ctx": other},
            device_id_type=MESH,
        )

    def part_copy(src, slot, other):
        return pltpu.make_async_remote_copy(
            src_ref=part_out.at[src],
            dst_ref=part_in.at[slot],
            send_sem=p_send.at[src],
            recv_sem=p_recv.at[slot],
            device_id={"ctx": other},
            device_id_type=MESH,
        )

    for t in range(1, n_ctx):
        @pl.when(me + t < n_ctx)
        def _():
            kv_copy(0, me, me + t).start()
            kv_copy(1, me, me + t).start()

    for load in loads:
        load.wait()

    gcol_s[...] = jnp.broadcast_to(qg_v[...], (HD, HD)).T
    for h in range(heads):
        hs = slice(h * HD, (h + 1) * HD)
        q_h = q_v[:, hs].T.astype(F32)
        inv = lax.rsqrt(jnp.mean(q_h * q_h, axis=0, keepdims=True) + 1e-06)
        unit = q_h * inv
        norm = (unit * gcol_s[...]).astype(BF16)
        unit_t[:, hs] = unit
        inv_s[:, hs] = inv
        qn_t[:, hs] = norm
        qn_s[h * rows:(h + 1) * rows, :] = norm.T
        gt = g_v[:, hs].T
        g_t[:, hs] = gt
        delta_s[:, hs] = jnp.sum(gt.astype(F32) * o_v[:, hs].T.astype(F32), axis=0, keepdims=True)
        lt2_s[:, hs] = lt_v[h:h + 1, :] * LOG2E

    def k_parts(b, c):
        x = kbuf[b, :, c * HD:(c + 1) * HD].astype(F32)
        inv = lax.rsqrt(jnp.mean(x * x, axis=-1, keepdims=True) + 1e-06)
        return x * inv, inv

    def block(b, diagonal):
        ksum = jnp.zeros((1, HD), F32)
        for c in range(kv_count):
            cs = slice(c * HD, (c + 1) * HD)
            k_unit, _ = k_parts(b, c)
            kn = (k_unit * kg_v[...]).astype(BF16)
            kn_t = kn.T
            vv = vbuf[b, :, cs]
            dk = jnp.zeros((rows, HD), F32)
            dv = jnp.zeros((rows, HD), F32)
            if diagonal:
                key_pos = lax.broadcasted_iota(jnp.int32, (rows, chunk * rows), 0)
                query_pos = lax.rem(
                    lax.broadcasted_iota(jnp.int32, (rows, chunk * rows), 1), rows
                )
                causal = query_pos >= key_pos
            for j in range(group // chunk):
                h = c * group + j * chunk
                sl = slice(h * HD, (h + chunk) * HD)
                s = dot(kn, qn_t[:, sl])
                p = jnp.exp2(s * (scale * LOG2E) - lt2_s[:, sl])
                if diagonal:
                    p = jnp.where(causal, p, 0.0)
                dp = dot(vv, g_t[:, sl])
                ds = (p * (dp - delta_s[:, sl])).astype(BF16)
                g_nat = jnp.concatenate(
                    [g_v[:, (h + i) * HD:(h + i + 1) * HD] for i in range(chunk)], axis=0
                )
                dv += dot(p.astype(BF16), g_nat)
                dk += dot(ds, qn_s[h * rows:(h + chunk) * rows, :])
                dq = dot(kn_t, ds)
                if diagonal:
                    dq_t[:, sl] = dq
                else:
                    dq_t[:, sl] += dq
            dk = dk * scale
            ksum += jnp.sum(dk * k_unit, axis=0, keepdims=True)
            if diagonal:
                gk_ref[:, cs] = dk
                gv_ref[:, cs] = dv
            else:
                part_out[b, :, cs] = dk.astype(BF16)
                part_out[b, :, kv_width + c * HD:kv_width + (c + 1) * HD] = dv.astype(BF16)
        return ksum

    ksum_s[...] = block(me, True)

    def step(t, carry):
        b = me - 1 - t
        kv_copy(0, b, b).wait_recv()
        kv_copy(1, b, b).wait_recv()
        ksum_s[...] += block(b, False)
        part_copy(b, me, b).start()
        return carry

    lax.fori_loop(0, me, step, 0)

    q_acc = jnp.zeros((HD, rows), F32)
    for h in range(heads):
        hs = slice(h * HD, (h + 1) * HD)
        gn = dq_t[:, hs] * scale
        unit = unit_t[:, hs]
        q_acc += gn * unit
        gp = gn * gcol_s[...]
        mean = jnp.mean(gp * unit, axis=0, keepdims=True)
        gq_ref[:, hs] = ((gp - unit * mean) * inv_s[:, hs]).T

    def gain_copy(buf, slot, send_sem, recv_sem, device_id):
        return pltpu.make_async_remote_copy(
            src_ref=buf.at[slot],
            dst_ref=buf.at[slot],
            send_sem=send_sem,
            recv_sem=recv_sem.at[slot],
            device_id=device_id,
            device_id_type=MESH,
        )

    buf_a[my_dp] = jnp.concatenate(
        [
            jnp.sum(q_acc.T, axis=0, keepdims=True), ksum_s[...],
            jnp.zeros((6, HD), F32),
        ],
        axis=0,
    )
    sent_a = []
    for t in range(1, n_dp):
        other = lax.rem(my_dp + t, n_dp)
        copy = gain_copy(buf_a, my_dp, a_send.at[t], a_recv, {"dp": other})
        copy.start()
        sent_a.append(copy)
    for t in range(1, n_dp):
        other = lax.rem(my_dp + t, n_dp)
        gain_copy(buf_a, other, a_send.at[t], a_recv, {"dp": other}).wait_recv()
    buf_b[my_plane] = jnp.sum(buf_a[...], axis=0)
    sent_b = []
    for t in range(1, n_plane):
        copy = gain_copy(buf_b, my_plane, b_send.at[t], b_recv, plane_id(t)[1])
        copy.start()
        sent_b.append(copy)

    def add_parts(a, carry):
        part_copy(a, a, a).wait_recv()
        gk_ref[...] += part_in[a, :, :kv_width].astype(F32)
        gv_ref[...] += part_in[a, :, kv_width:].astype(F32)
        return carry

    lax.fori_loop(me + 1, n_ctx, add_parts, 0)
    for c in range(kv_count):
        cs = slice(c * HD, (c + 1) * HD)
        unit, inv = k_parts(me, c)
        gp = gk_ref[:, cs] * kg_v[...]
        gk_ref[:, cs] = (gp - unit * jnp.mean(gp * unit, axis=-1, keepdims=True)) * inv

    for t in range(1, n_plane):
        slot, device_id = plane_id(t)
        gain_copy(buf_b, slot, b_send.at[t], b_recv, device_id).wait_recv()
    gain_ref[...] = jnp.sum(buf_b[...], axis=0)[:2] * gain_scale

    for copy in sent_a + sent_b:
        copy.wait_send()
    for t in range(1, n_ctx):
        @pl.when(me + t < n_ctx)
        def _():
            kv_copy(0, me, me + t).wait_send()
            kv_copy(1, me, me + t).wait_send()

        @pl.when(me - t >= 0)
        def _():
            part_copy(me - t, me, me - t).wait_send()


def local(query_raw, key_raw, value_rows, attn_out, out_grad, log_totals, query_gain, key_gain):
    n_ctx = lax.axis_size("ctx")
    n_head = lax.axis_size("head")
    n_dp = lax.axis_size("dp")
    batch, rows, width = query_raw.shape
    kv_width = key_raw.shape[2]
    heads = width // HD
    n_plane = n_ctx * n_head
    pair_count = batch * n_dp * rows * n_ctx * heads * n_head
    vmem = pltpu.VMEM
    dma = pltpu.SemaphoreType.DMA
    flops = 10 * heads * rows * rows * HD * n_ctx
    gq, gk, gv, gains = pl.pallas_call(
        functools.partial(kernel, n_ctx, n_head, n_dp, 1.0 / math.sqrt(pair_count)),
        out_shape=(
            jax.ShapeDtypeStruct((rows, width), F32),
            jax.ShapeDtypeStruct((rows, kv_width), F32),
            jax.ShapeDtypeStruct((rows, kv_width), F32),
            jax.ShapeDtypeStruct((2, HD), F32),
        ),
        in_specs=[pl.BlockSpec(memory_space=pl.ANY)] * 8,
        out_specs=tuple([pl.BlockSpec(memory_space=pltpu.VMEM)] * 4),
        scratch_shapes=[
            vmem((rows, width), BF16), vmem((rows, width), BF16), vmem((rows, width), BF16),
            vmem((heads, rows), F32), vmem((1, HD), F32), vmem((1, HD), F32),
            vmem((n_ctx, rows, kv_width), BF16), vmem((n_ctx, rows, kv_width), BF16),
            vmem((n_ctx, rows, 2 * kv_width), BF16), vmem((n_ctx, rows, 2 * kv_width), BF16),
            vmem((HD, heads * rows), F32), vmem((1, heads * rows), F32),
            vmem((HD, heads * rows), BF16), vmem((heads * rows, HD), BF16),
            vmem((HD, heads * rows), BF16), vmem((1, heads * rows), F32),
            vmem((1, heads * rows), F32), vmem((HD, heads * rows), F32),
            vmem((HD, HD), F32), vmem((1, HD), F32),
            vmem((n_dp, 8, HD), F32), vmem((n_plane, 8, HD), F32),
            dma((8,)), dma((2, n_ctx)), dma((2, n_ctx)), dma((n_ctx,)), dma((n_ctx,)),
            dma((n_dp,)), dma((n_dp,)), dma((n_plane,)), dma((n_plane,)),
        ],
        compiler_params=pltpu.CompilerParams(
            collective_id=0, has_side_effects=True, vmem_limit_bytes=32 * 1024 * 1024
        ),
        cost_estimate=pl.CostEstimate(
            flops=flops, bytes_accessed=4 * rows * width * 4, transcendentals=heads * rows * rows * n_ctx
        ),
    )(
        query_raw[0], key_raw[0], value_rows[0], attn_out[0], out_grad[0], log_totals[0],
        query_gain.reshape(1, HD), key_gain.reshape(1, HD),
    )
    return gq[None], gk[None], gv[None], gains


def solution(mesh):
    return jax.shard_map(
        local,
        mesh=mesh,
        in_specs=(
            P("dp", "ctx", "head"),
            P("dp", "ctx", "head"),
            P("dp", "ctx", "head"),
            P("dp", "ctx", "head"),
            P("dp", "ctx", "head"),
            P("dp", "head", "ctx"),
            P(),
            P(),
        ),
        out_specs=(P("dp", "ctx", "head"), P("dp", "ctx", "head"), P("dp", "ctx", "head"), P()),
        check_vma=False,
    )
```

```python
import functools
import math

import jax
import jax.numpy as jnp
from jax import lax
from jax.experimental import pallas as pl
from jax.experimental.pallas import tpu as pltpu
from jax.sharding import PartitionSpec as P

HD = 128
F32 = jnp.float32
BF16 = jnp.bfloat16
MESH = pl.DeviceIdType.MESH
LOG2E = math.log2(math.e)


def dot(a, b):
    return jnp.dot(a, b, preferred_element_type=F32)


def kernel(
    n_ctx, n_head, n_dp, gain_scale,
    q_hbm, k_hbm, v_hbm, o_hbm, g_hbm, lt_hbm, qg_hbm, kg_hbm,
    gq_ref, gk_ref, gv_ref, gain_ref,
    q_v, o_v, g_v, lt_v, qg_v, kg_v,
    kbuf, vbuf, part_out, part_in,
    unit_t, inv_s, qn_t, qn_s, g_t, delta_s, lt2_s, dq_t, gcol_s, ksum_s, buf_a, buf_b,
    in_sem, kv_send, kv_recv, p_send, p_recv, a_send, a_recv, b_send, b_recv,
):
    rows, width = q_v.shape
    heads = width // HD
    kv_width = k_hbm.shape[1]
    kv_count = kv_width // HD
    group = heads // kv_count
    chunk = math.gcd(group, 2)
    scale = 1.0 / math.sqrt(HD)
    me = lax.axis_index("ctx")
    my_head = lax.axis_index("head")
    my_dp = lax.axis_index("dp")
    n_plane = n_ctx * n_head
    my_plane = me * n_head + my_head

    loads = [
        pltpu.make_async_copy(src, dst, in_sem.at[i])
        for i, (src, dst) in enumerate(
            [
                (k_hbm, kbuf.at[me]), (v_hbm, vbuf.at[me]), (lt_hbm, lt_v), (qg_hbm, qg_v),
                (kg_hbm, kg_v), (q_hbm, q_v), (g_hbm, g_v), (o_hbm, o_v),
            ]
        )
    ]
    for load in loads:
        load.start()

    def plane_id(t):
        p = lax.rem(my_plane + t, n_plane)
        return p, {"ctx": p // n_head, "head": lax.rem(p, n_head)}

    barrier = pltpu.get_barrier_semaphore()
    for t in range(1, n_plane):
        pl.semaphore_signal(barrier, inc=1, device_id=plane_id(t)[1], device_id_type=MESH)
    for t in range(1, n_dp):
        pl.semaphore_signal(
            barrier, inc=1, device_id={"dp": lax.rem(my_dp + t, n_dp)}, device_id_type=MESH
        )
    pl.semaphore_wait(barrier, n_plane + n_dp - 2)

    def kv_copy(which, slot, other):
        return pltpu.make_async_remote_copy(
            src_ref=(k_hbm, v_hbm)[which],
            dst_ref=(kbuf, vbuf)[which].at[slot],
            send_sem=kv_send.at[which, other],
            recv_sem=kv_recv.at[which, slot],
            device_id={"ctx": other},
            device_id_type=MESH,
        )

    def part_copy(src, slot, other):
        return pltpu.make_async_remote_copy(
            src_ref=part_out.at[src],
            dst_ref=part_in.at[slot],
            send_sem=p_send.at[src],
            recv_sem=p_recv.at[slot],
            device_id={"ctx": other},
            device_id_type=MESH,
        )

    for t in range(1, n_ctx):
        @pl.when(me + t < n_ctx)
        def _():
            kv_copy(0, me, me + t).start()
            kv_copy(1, me, me + t).start()

    for load in loads:
        load.wait()

    gcol_s[...] = jnp.broadcast_to(qg_v[...], (HD, HD)).T
    for h in range(heads):
        hs = slice(h * HD, (h + 1) * HD)
        q_h = q_v[:, hs].T.astype(F32)
        inv = lax.rsqrt(jnp.mean(q_h * q_h, axis=0, keepdims=True) + 1e-06)
        unit = q_h * inv
        norm = (unit * gcol_s[...]).astype(BF16)
        unit_t[:, hs] = unit
        inv_s[:, hs] = inv
        qn_t[:, hs] = norm
        qn_s[h * rows:(h + 1) * rows, :] = norm.T
        gt = g_v[:, hs].T
        g_t[:, hs] = gt
        delta_s[:, hs] = jnp.sum(gt.astype(F32) * o_v[:, hs].T.astype(F32), axis=0, keepdims=True)
        lt2_s[:, hs] = lt_v[h:h + 1, :] * LOG2E

    def k_parts(b, c):
        x = kbuf[b, :, c * HD:(c + 1) * HD].astype(F32)
        inv = lax.rsqrt(jnp.mean(x * x, axis=-1, keepdims=True) + 1e-06)
        return x * inv, inv

    def block(b, diagonal):
        ksum = jnp.zeros((1, HD), F32)
        for c in range(kv_count):
            cs = slice(c * HD, (c + 1) * HD)
            k_unit, _ = k_parts(b, c)
            kn = (k_unit * kg_v[...]).astype(BF16)
            kn_t = kn.T
            vv = vbuf[b, :, cs]
            dk = jnp.zeros((rows, HD), F32)
            dv = jnp.zeros((rows, HD), F32)
            if diagonal:
                key_pos = lax.broadcasted_iota(jnp.int32, (rows, chunk * rows), 0)
                query_pos = lax.rem(
                    lax.broadcasted_iota(jnp.int32, (rows, chunk * rows), 1), rows
                )
                causal = query_pos >= key_pos
            for j in range(group // chunk):
                h = c * group + j * chunk
                sl = slice(h * HD, (h + chunk) * HD)
                s = dot(kn, qn_t[:, sl])
                p = jnp.exp2(s * (scale * LOG2E) - lt2_s[:, sl])
                if diagonal:
                    p = jnp.where(causal, p, 0.0)
                dp = dot(vv, g_t[:, sl])
                ds = (p * (dp - delta_s[:, sl])).astype(BF16)
                g_nat = jnp.concatenate(
                    [g_v[:, (h + i) * HD:(h + i + 1) * HD] for i in range(chunk)], axis=0
                )
                dv += dot(p.astype(BF16), g_nat)
                dk += dot(ds, qn_s[h * rows:(h + chunk) * rows, :])
                dq = dot(kn_t, ds)
                if diagonal:
                    dq_t[:, sl] = dq
                else:
                    dq_t[:, sl] += dq
            dk = dk * scale
            ksum += jnp.sum(dk * k_unit, axis=0, keepdims=True)
            if diagonal:
                gk_ref[:, cs] = dk
                gv_ref[:, cs] = dv
            else:
                part_out[b, :, cs] = dk.astype(BF16)
                part_out[b, :, kv_width + c * HD:kv_width + (c + 1) * HD] = dv.astype(BF16)
        return ksum

    ksum_s[...] = block(me, True)

    def step(t, carry):
        b = me - 1 - t
        kv_copy(0, b, b).wait_recv()
        kv_copy(1, b, b).wait_recv()
        ksum_s[...] += block(b, False)
        part_copy(b, me, b).start()
        return carry

    lax.fori_loop(0, me, step, 0)

    q_acc = jnp.zeros((HD, rows), F32)
    for h in range(heads):
        hs = slice(h * HD, (h + 1) * HD)
        gn = dq_t[:, hs] * scale
        unit = unit_t[:, hs]
        q_acc += gn * unit
        gp = gn * gcol_s[...]
        mean = jnp.mean(gp * unit, axis=0, keepdims=True)
        gq_ref[:, hs] = ((gp - unit * mean) * inv_s[:, hs]).T

    def gain_copy(buf, slot, send_sem, recv_sem, device_id):
        return pltpu.make_async_remote_copy(
            src_ref=buf.at[slot],
            dst_ref=buf.at[slot],
            send_sem=send_sem,
            recv_sem=recv_sem.at[slot],
            device_id=device_id,
            device_id_type=MESH,
        )

    buf_a[my_dp] = jnp.concatenate(
        [
            jnp.sum(q_acc.T, axis=0, keepdims=True), ksum_s[...],
            jnp.zeros((6, HD), F32),
        ],
        axis=0,
    )
    sent_a = []
    for t in range(1, n_dp):
        other = lax.rem(my_dp + t, n_dp)
        copy = gain_copy(buf_a, my_dp, a_send.at[t], a_recv, {"dp": other})
        copy.start()
        sent_a.append(copy)
    for t in range(1, n_dp):
        other = lax.rem(my_dp + t, n_dp)
        gain_copy(buf_a, other, a_send.at[t], a_recv, {"dp": other}).wait_recv()
    buf_b[my_plane] = jnp.sum(buf_a[...], axis=0)
    sent_b = []
    for t in range(1, n_plane):
        copy = gain_copy(buf_b, my_plane, b_send.at[t], b_recv, plane_id(t)[1])
        copy.start()
        sent_b.append(copy)

    def add_parts(a, carry):
        part_copy(a, a, a).wait_recv()
        gk_ref[...] += part_in[a, :, :kv_width].astype(F32)
        gv_ref[...] += part_in[a, :, kv_width:].astype(F32)
        return carry

    lax.fori_loop(me + 1, n_ctx, add_parts, 0)
    for c in range(kv_count):
        cs = slice(c * HD, (c + 1) * HD)
        unit, inv = k_parts(me, c)
        gp = gk_ref[:, cs] * kg_v[...]
        gk_ref[:, cs] = (gp - unit * jnp.mean(gp * unit, axis=-1, keepdims=True)) * inv

    for t in range(1, n_plane):
        slot, device_id = plane_id(t)
        gain_copy(buf_b, slot, b_send.at[t], b_recv, device_id).wait_recv()
    gain_ref[...] = jnp.sum(buf_b[...], axis=0)[:2] * gain_scale

    for copy in sent_a + sent_b:
        copy.wait_send()
    for t in range(1, n_ctx):
        @pl.when(me + t < n_ctx)
        def _():
            kv_copy(0, me, me + t).wait_send()
            kv_copy(1, me, me + t).wait_send()

        @pl.when(me - t >= 0)
        def _():
            part_copy(me - t, me, me - t).wait_send()


def hold(*xs):
    return [pltpu.with_memory_space_constraint(x, pltpu.HBM) for x in xs]


def write_out(*refs):
    sem = refs[-1]
    half = len(refs) // 2
    copies = []
    for i, (src, dst) in enumerate(zip(refs[:half], refs[half:-1])):
        rows = src.shape[0]
        cuts = 4 if rows % 64 == 0 and src.shape[1] > 512 else 1
        step = rows // cuts
        for c in range(cuts):
            part = pl.ds(c * step, step)
            copies.append(pltpu.make_async_copy(src.at[part], dst.at[part], sem.at[len(copies)]))
    for copy in copies:
        copy.start()
    for copy in copies:
        copy.wait()


def local(query_raw, key_raw, value_rows, attn_out, out_grad, log_totals, query_gain, key_gain):
    n_ctx = lax.axis_size("ctx")
    n_head = lax.axis_size("head")
    n_dp = lax.axis_size("dp")
    batch, rows, width = query_raw.shape
    kv_width = key_raw.shape[2]
    heads = width // HD
    n_plane = n_ctx * n_head
    pair_count = batch * n_dp * rows * n_ctx * heads * n_head
    vmem = pltpu.VMEM
    dma = pltpu.SemaphoreType.DMA
    flops = 10 * heads * rows * rows * HD * n_ctx
    gq, gk, gv, gains = pl.pallas_call(
        functools.partial(kernel, n_ctx, n_head, n_dp, 1.0 / math.sqrt(pair_count)),
        out_shape=(
            jax.ShapeDtypeStruct((rows, width), F32),
            jax.ShapeDtypeStruct((rows, kv_width), F32),
            jax.ShapeDtypeStruct((rows, kv_width), F32),
            jax.ShapeDtypeStruct((2, HD), F32),
        ),
        in_specs=[pl.BlockSpec(memory_space=pltpu.HBM)] * 8,
        out_specs=tuple([pl.BlockSpec(memory_space=pltpu.VMEM)] * 4),
        scratch_shapes=[
            vmem((rows, width), BF16), vmem((rows, width), BF16), vmem((rows, width), BF16),
            vmem((heads, rows), F32), vmem((1, HD), F32), vmem((1, HD), F32),
            vmem((n_ctx, rows, kv_width), BF16), vmem((n_ctx, rows, kv_width), BF16),
            vmem((n_ctx, rows, 2 * kv_width), BF16), vmem((n_ctx, rows, 2 * kv_width), BF16),
            vmem((HD, heads * rows), F32), vmem((1, heads * rows), F32),
            vmem((HD, heads * rows), BF16), vmem((heads * rows, HD), BF16),
            vmem((HD, heads * rows), BF16), vmem((1, heads * rows), F32),
            vmem((1, heads * rows), F32), vmem((HD, heads * rows), F32),
            vmem((HD, HD), F32), vmem((1, HD), F32),
            vmem((n_dp, 8, HD), F32), vmem((n_plane, 8, HD), F32),
            dma((8,)), dma((2, n_ctx)), dma((2, n_ctx)), dma((n_ctx,)), dma((n_ctx,)),
            dma((n_dp,)), dma((n_dp,)), dma((n_plane,)), dma((n_plane,)),
        ],
        compiler_params=pltpu.CompilerParams(
            collective_id=0, has_side_effects=True, vmem_limit_bytes=48 * 1024 * 1024
        ),
        cost_estimate=pl.CostEstimate(
            flops=flops, bytes_accessed=4 * rows * width * 4, transcendentals=heads * rows * rows * n_ctx
        ),
    )(*hold(
        query_raw[0], key_raw[0], value_rows[0], attn_out[0], out_grad[0], log_totals[0],
        query_gain.reshape(1, HD), key_gain.reshape(1, HD),
    ))
    results = (gq, gk, gv, gains)
    gq, gk, gv, gains = pl.pallas_call(
        write_out,
        out_shape=tuple(jax.ShapeDtypeStruct(x.shape, x.dtype) for x in results),
        in_specs=[pl.BlockSpec(memory_space=pl.ANY)] * 4,
        out_specs=tuple([pl.BlockSpec(memory_space=pl.ANY)] * 4),
        scratch_shapes=[dma((16,))],
        compiler_params=pltpu.CompilerParams(vmem_limit_bytes=1024 * 1024),
    )(*results)
    return gq[None], gk[None], gv[None], gains


def solution(mesh):
    return jax.shard_map(
        local,
        mesh=mesh,
        in_specs=(
            P("dp", "ctx", "head"),
            P("dp", "ctx", "head"),
            P("dp", "ctx", "head"),
            P("dp", "ctx", "head"),
            P("dp", "ctx", "head"),
            P("dp", "head", "ctx"),
            P(),
            P(),
        ),
        out_specs=(P("dp", "ctx", "head"), P("dp", "ctx", "head"), P("dp", "ctx", "head"), P()),
        check_vma=False,
    )
```

```python
import functools
import math

import jax
import jax.numpy as jnp
from jax import lax
from jax.experimental import pallas as pl
from jax.experimental.pallas import tpu as pltpu
from jax.sharding import PartitionSpec as P

HD = 128
F32 = jnp.float32
BF16 = jnp.bfloat16
MESH = pl.DeviceIdType.MESH
LOG2E = math.log2(math.e)


def dot(a, b):
    return jnp.dot(a, b, preferred_element_type=F32)


def kernel(
    n_ctx, n_head, n_dp, gain_scale,
    q_hbm, k_hbm, v_hbm, o_hbm, g_hbm, lt_hbm, qg_hbm, kg_hbm,
    gq_ref, gk_ref, gv_ref, gain_ref,
    q_v, o_v, g_v, lt_v, qg_v, kg_v,
    kbuf, vbuf, part_out, part_in,
    unit_t, inv_s, qn_t, qn_s, g_t, delta_s, lt2_s, dq_t, gcol_s, ksum_s, buf_a, buf_b,
    in_sem, kv_send, kv_recv, p_send, p_recv, a_send, a_recv, b_send, b_recv,
):
    rows, width = q_v.shape
    heads = width // HD
    kv_width = k_hbm.shape[1]
    kv_count = kv_width // HD
    group = heads // kv_count
    chunk = math.gcd(group, 2)
    scale = 1.0 / math.sqrt(HD)
    me = lax.axis_index("ctx")
    my_head = lax.axis_index("head")
    my_dp = lax.axis_index("dp")
    n_plane = n_ctx * n_head
    my_plane = me * n_head + my_head

    loads = [
        pltpu.make_async_copy(src, dst, in_sem.at[i])
        for i, (src, dst) in enumerate(
            [
                (k_hbm, kbuf.at[me]), (v_hbm, vbuf.at[me]), (lt_hbm, lt_v), (qg_hbm, qg_v),
                (kg_hbm, kg_v), (q_hbm, q_v), (g_hbm, g_v), (o_hbm, o_v),
            ]
        )
    ]
    for load in loads:
        load.start()

    def plane_id(t):
        p = lax.rem(my_plane + t, n_plane)
        return p, {"ctx": p // n_head, "head": lax.rem(p, n_head)}

    barrier = pltpu.get_barrier_semaphore()
    for t in range(1, n_plane):
        pl.semaphore_signal(barrier, inc=1, device_id=plane_id(t)[1], device_id_type=MESH)
    for t in range(1, n_dp):
        pl.semaphore_signal(
            barrier, inc=1, device_id={"dp": lax.rem(my_dp + t, n_dp)}, device_id_type=MESH
        )
    pl.semaphore_wait(barrier, n_plane + n_dp - 2)

    def kv_copy(which, slot, other):
        return pltpu.make_async_remote_copy(
            src_ref=(kbuf, vbuf)[which].at[slot],
            dst_ref=(kbuf, vbuf)[which].at[slot],
            send_sem=kv_send.at[which, other],
            recv_sem=kv_recv.at[which, slot],
            device_id={"ctx": other},
            device_id_type=MESH,
        )

    def part_copy(src, slot, other):
        return pltpu.make_async_remote_copy(
            src_ref=part_out.at[src],
            dst_ref=part_in.at[slot],
            send_sem=p_send.at[src],
            recv_sem=p_recv.at[slot],
            device_id={"ctx": other},
            device_id_type=MESH,
        )

    for which in range(2):
        loads[which].wait()
        for t in range(1, n_ctx):
            @pl.when(me + t < n_ctx)
            def _():
                kv_copy(which, me, me + t).start()

    for load in loads[2:]:
        load.wait()

    gcol_s[...] = jnp.broadcast_to(qg_v[...], (HD, HD)).T
    for h in range(heads):
        hs = slice(h * HD, (h + 1) * HD)
        q_h = q_v[:, hs].T.astype(F32)
        inv = lax.rsqrt(jnp.mean(q_h * q_h, axis=0, keepdims=True) + 1e-06)
        unit = q_h * inv
        norm = (unit * gcol_s[...]).astype(BF16)
        unit_t[:, hs] = unit
        inv_s[:, hs] = inv
        qn_t[:, hs] = norm
        qn_s[h * rows:(h + 1) * rows, :] = norm.T
        gt = g_v[:, hs].T
        g_t[:, hs] = gt
        delta_s[:, hs] = jnp.sum(gt.astype(F32) * o_v[:, hs].T.astype(F32), axis=0, keepdims=True)
        lt2_s[:, hs] = lt_v[h:h + 1, :] * LOG2E

    def k_parts(b, c):
        x = kbuf[b, :, c * HD:(c + 1) * HD].astype(F32)
        inv = lax.rsqrt(jnp.mean(x * x, axis=-1, keepdims=True) + 1e-06)
        return x * inv, inv

    def block(b, diagonal):
        ksum = jnp.zeros((1, HD), F32)
        for c in range(kv_count):
            cs = slice(c * HD, (c + 1) * HD)
            k_unit, _ = k_parts(b, c)
            kn = (k_unit * kg_v[...]).astype(BF16)
            kn_t = kn.T
            vv = vbuf[b, :, cs]
            dk = jnp.zeros((rows, HD), F32)
            dv = jnp.zeros((rows, HD), F32)
            if diagonal:
                key_pos = lax.broadcasted_iota(jnp.int32, (rows, chunk * rows), 0)
                query_pos = lax.rem(
                    lax.broadcasted_iota(jnp.int32, (rows, chunk * rows), 1), rows
                )
                causal = query_pos >= key_pos
            for j in range(group // chunk):
                h = c * group + j * chunk
                sl = slice(h * HD, (h + chunk) * HD)
                s = dot(kn, qn_t[:, sl])
                p = jnp.exp2(s * (scale * LOG2E) - lt2_s[:, sl])
                if diagonal:
                    p = jnp.where(causal, p, 0.0)
                dp = dot(vv, g_t[:, sl])
                ds = (p * (dp - delta_s[:, sl])).astype(BF16)
                g_nat = jnp.concatenate(
                    [g_v[:, (h + i) * HD:(h + i + 1) * HD] for i in range(chunk)], axis=0
                )
                dv += dot(p.astype(BF16), g_nat)
                dk += dot(ds, qn_s[h * rows:(h + chunk) * rows, :])
                dq = dot(kn_t, ds)
                if diagonal:
                    dq_t[:, sl] = dq
                else:
                    dq_t[:, sl] += dq
            dk = dk * scale
            ksum += jnp.sum(dk * k_unit, axis=0, keepdims=True)
            if diagonal:
                gk_ref[:, cs] = dk
                gv_ref[:, cs] = dv
            else:
                part_out[b, :, cs] = dk.astype(BF16)
                part_out[b, :, kv_width + c * HD:kv_width + (c + 1) * HD] = dv.astype(BF16)
        return ksum

    ksum_s[...] = block(me, True)

    def step(t, carry):
        b = me - 1 - t
        kv_copy(0, b, b).wait_recv()
        kv_copy(1, b, b).wait_recv()
        ksum_s[...] += block(b, False)
        part_copy(b, me, b).start()
        return carry

    lax.fori_loop(0, me, step, 0)

    q_acc = jnp.zeros((HD, rows), F32)
    for h in range(heads):
        hs = slice(h * HD, (h + 1) * HD)
        gn = dq_t[:, hs] * scale
        unit = unit_t[:, hs]
        q_acc += gn * unit
        gp = gn * gcol_s[...]
        mean = jnp.mean(gp * unit, axis=0, keepdims=True)
        gq_ref[:, hs] = ((gp - unit * mean) * inv_s[:, hs]).T

    def gain_copy(buf, slot, send_sem, recv_sem, device_id):
        return pltpu.make_async_remote_copy(
            src_ref=buf.at[slot],
            dst_ref=buf.at[slot],
            send_sem=send_sem,
            recv_sem=recv_sem.at[slot],
            device_id=device_id,
            device_id_type=MESH,
        )

    buf_a[my_dp] = jnp.concatenate(
        [
            jnp.sum(q_acc.T, axis=0, keepdims=True), ksum_s[...],
            jnp.zeros((6, HD), F32),
        ],
        axis=0,
    )
    sent_a = []
    for t in range(1, n_dp):
        other = lax.rem(my_dp + t, n_dp)
        copy = gain_copy(buf_a, my_dp, a_send.at[t], a_recv, {"dp": other})
        copy.start()
        sent_a.append(copy)
    for t in range(1, n_dp):
        other = lax.rem(my_dp + t, n_dp)
        gain_copy(buf_a, other, a_send.at[t], a_recv, {"dp": other}).wait_recv()
    buf_b[my_plane] = jnp.sum(buf_a[...], axis=0)
    sent_b = []
    for t in range(1, n_plane):
        copy = gain_copy(buf_b, my_plane, b_send.at[t], b_recv, plane_id(t)[1])
        copy.start()
        sent_b.append(copy)

    def add_parts(a, carry):
        part_copy(a, a, a).wait_recv()
        gk_ref[...] += part_in[a, :, :kv_width].astype(F32)
        gv_ref[...] += part_in[a, :, kv_width:].astype(F32)
        return carry

    lax.fori_loop(me + 1, n_ctx, add_parts, 0)
    for c in range(kv_count):
        cs = slice(c * HD, (c + 1) * HD)
        unit, inv = k_parts(me, c)
        gp = gk_ref[:, cs] * kg_v[...]
        gk_ref[:, cs] = (gp - unit * jnp.mean(gp * unit, axis=-1, keepdims=True)) * inv

    for t in range(1, n_plane):
        slot, device_id = plane_id(t)
        gain_copy(buf_b, slot, b_send.at[t], b_recv, device_id).wait_recv()
    gain_ref[...] = jnp.sum(buf_b[...], axis=0)[:2] * gain_scale

    for copy in sent_a + sent_b:
        copy.wait_send()
    for t in range(1, n_ctx):
        @pl.when(me + t < n_ctx)
        def _():
            kv_copy(0, me, me + t).wait_send()
            kv_copy(1, me, me + t).wait_send()

        @pl.when(me - t >= 0)
        def _():
            part_copy(me - t, me, me - t).wait_send()


def hold(*xs):
    return [pltpu.with_memory_space_constraint(x, pltpu.HBM) for x in xs]


def write_out(*refs):
    sem = refs[-1]
    half = len(refs) // 2
    copies = []
    for i, (src, dst) in enumerate(zip(refs[:half], refs[half:-1])):
        rows = src.shape[0]
        cuts = 4 if rows % 64 == 0 and src.shape[1] > 512 else 1
        step = rows // cuts
        for c in range(cuts):
            part = pl.ds(c * step, step)
            copies.append(pltpu.make_async_copy(src.at[part], dst.at[part], sem.at[len(copies)]))
    for copy in copies:
        copy.start()
    for copy in copies:
        copy.wait()


def local(query_raw, key_raw, value_rows, attn_out, out_grad, log_totals, query_gain, key_gain):
    n_ctx = lax.axis_size("ctx")
    n_head = lax.axis_size("head")
    n_dp = lax.axis_size("dp")
    batch, rows, width = query_raw.shape
    kv_width = key_raw.shape[2]
    heads = width // HD
    n_plane = n_ctx * n_head
    pair_count = batch * n_dp * rows * n_ctx * heads * n_head
    vmem = pltpu.VMEM
    dma = pltpu.SemaphoreType.DMA
    flops = 10 * heads * rows * rows * HD * n_ctx
    gq, gk, gv, gains = pl.pallas_call(
        functools.partial(kernel, n_ctx, n_head, n_dp, 1.0 / math.sqrt(pair_count)),
        out_shape=(
            jax.ShapeDtypeStruct((rows, width), F32),
            jax.ShapeDtypeStruct((rows, kv_width), F32),
            jax.ShapeDtypeStruct((rows, kv_width), F32),
            jax.ShapeDtypeStruct((2, HD), F32),
        ),
        in_specs=[pl.BlockSpec(memory_space=pltpu.HBM)] * 8,
        out_specs=tuple([pl.BlockSpec(memory_space=pltpu.VMEM)] * 4),
        scratch_shapes=[
            vmem((rows, width), BF16), vmem((rows, width), BF16), vmem((rows, width), BF16),
            vmem((heads, rows), F32), vmem((1, HD), F32), vmem((1, HD), F32),
            vmem((n_ctx, rows, kv_width), BF16), vmem((n_ctx, rows, kv_width), BF16),
            vmem((n_ctx, rows, 2 * kv_width), BF16), vmem((n_ctx, rows, 2 * kv_width), BF16),
            vmem((HD, heads * rows), F32), vmem((1, heads * rows), F32),
            vmem((HD, heads * rows), BF16), vmem((heads * rows, HD), BF16),
            vmem((HD, heads * rows), BF16), vmem((1, heads * rows), F32),
            vmem((1, heads * rows), F32), vmem((HD, heads * rows), F32),
            vmem((HD, HD), F32), vmem((1, HD), F32),
            vmem((n_dp, 8, HD), F32), vmem((n_plane, 8, HD), F32),
            dma((8,)), dma((2, n_ctx)), dma((2, n_ctx)), dma((n_ctx,)), dma((n_ctx,)),
            dma((n_dp,)), dma((n_dp,)), dma((n_plane,)), dma((n_plane,)),
        ],
        compiler_params=pltpu.CompilerParams(
            collective_id=0, has_side_effects=True, vmem_limit_bytes=48 * 1024 * 1024
        ),
        cost_estimate=pl.CostEstimate(
            flops=flops, bytes_accessed=4 * rows * width * 4, transcendentals=heads * rows * rows * n_ctx
        ),
    )(*hold(
        query_raw[0], key_raw[0], value_rows[0], attn_out[0], out_grad[0], log_totals[0],
        query_gain.reshape(1, HD), key_gain.reshape(1, HD),
    ))
    results = (gq, gk, gv, gains)
    gq, gk, gv, gains = pl.pallas_call(
        write_out,
        out_shape=tuple(jax.ShapeDtypeStruct(x.shape, x.dtype) for x in results),
        in_specs=[pl.BlockSpec(memory_space=pl.ANY)] * 4,
        out_specs=tuple([pl.BlockSpec(memory_space=pl.ANY)] * 4),
        scratch_shapes=[dma((16,))],
        compiler_params=pltpu.CompilerParams(vmem_limit_bytes=1024 * 1024),
    )(*results)
    return gq[None], gk[None], gv[None], gains


def solution(mesh):
    return jax.shard_map(
        local,
        mesh=mesh,
        in_specs=(
            P("dp", "ctx", "head"),
            P("dp", "ctx", "head"),
            P("dp", "ctx", "head"),
            P("dp", "ctx", "head"),
            P("dp", "ctx", "head"),
            P("dp", "head", "ctx"),
            P(),
            P(),
        ),
        out_specs=(P("dp", "ctx", "head"), P("dp", "ctx", "head"), P("dp", "ctx", "head"), P()),
        check_vma=False,
    )
```
